32 devices in a mesh: dp: 4 (over y, core), expert: 8 (over z, x).
Axes of the slice: x: 2, y: 2, z: 4, core: 2. Of those that a mesh axis runs over, the one named last changes fastest.
Arguments:
- tokens: bfloat16 [8192, 4096], P(('dp', 'expert')), may hold values from -6 to 6
- routes: int32 [8192, 2], P(('dp', 'expert')), may hold values from 0 to 7, all different within a row; in each aligned block of 256 rows (0 to 255, 256 to 511, ...) at most 128 rows name the same one
- route_weights: float32 [8192, 2], P(('dp', 'expert')), may hold values from 0.1 to 0.9
- placement: int32 [8], replicated, may hold values from 0 to 7, each once
- expert_weights: bfloat16 [8, 4096, 1024], P('expert', None, 'dp'), may hold values from -0.09375 to 0.09375
- grads: bfloat16 [8, 4096, 1024], P('expert', None, 'dp'), may hold values from -0.059814453 to 0.059814453
- first_moment: bfloat16 [8, 4096, 1024], P('expert', None, 'dp'), may hold values from -0.017944336 to 0.017944336
- second_moment: bfloat16 [8, 4096, 1024], P('expert', None, 'dp'), may hold values from 9.953976e-06 to 0.0009994507
Outputs:
- new_weights: bfloat16 [8, 4096, 1024], P('expert', None, 'dp')
- new_first: bfloat16 [8, 4096, 1024], P('expert', None, 'dp')
- new_second: bfloat16 [8, 4096, 1024], P('expert', None, 'dp')
- mixed: bfloat16 [8192, 1024], P(('dp', 'expert'))
The draws below stay inside these ranges and needn't reach their ends.
Inputs may be any that keep to these rules, and one draw needn't show every extreme that they name: `routes`: each token names two different experts; within the rows of one device no expert is named more than 128 times, a bound that some block reaches. `placement`: each expert appears exactly once.
All inputs are finite; a program needn't handle non-finite values.
Results may differ from the reference program's by a relative error of at most 0.0057.
Values may be sent and summed in bfloat16 or wider, within the bound.
No kernel may reach another device: no remote copies, remote signals or barrier semaphores. Data moves between devices by JAX's collectives and lax.ppermute only.
A program may use at most 192 MiB of HBM per device.

```python
import math
import jax
import jax.numpy as jnp
import numpy as np
from jax import lax

D = 4096
HID = 1024
TOK_DEV = 256
EXPERTS = 8
CAP = 128
TOKENS = 8192
N_DP = 4
N_EXPERT = 8


def level_of(stream_key, shape, cuts, least, largest):
    level = 1.0
    for axis_at, parts in cuts:
        heights = jax.random.uniform(jax.random.fold_in(jax.random.fold_in(stream_key, 6), axis_at), (parts,), jnp.float32, least / len(cuts), largest / len(cuts))
        level = level * jnp.repeat(jnp.exp(heights), shape[axis_at] // parts).reshape((-1,) + (1,) * (len(shape) - 1 - axis_at))
    return level


def routed_block(own_key, own, number, rows, number_of, top, reach, lean):
    order = jax.random.permutation(own_key, number_of)
    crowded, common = shares(number_of, rows * top, reach, lean, True), shares(number_of, rows * top, reach, lean, False)
    places = jnp.arange(number_of)

    def named(lengths, turn):
        used = int((lengths > 0).sum())
        fixed = max(1, used // 4)
        passed = fixed + (places - fixed + turn * (used - fixed)) % max(1, number_of - fixed)
        return jnp.zeros((number_of,), jnp.int32).at[order[jnp.where(places < fixed, places, passed)]].set(jnp.asarray(lengths, jnp.int32))

    lengths = jnp.where(number % 4 == 0, named(crowded, number // 4), named(common, number - number // 4 - 1))
    mixed = jax.random.permutation(jax.random.fold_in(own, 3), number_of)
    donor, receiver = mixed[0:number_of // 2 * 2:2], mixed[1:number_of // 2 * 2:2]
    slack = jnp.minimum(lengths[donor] - 1, reach - lengths[receiver]) // 2
    slack = jnp.where((donor == order[0]) | (receiver == order[0]) | (lengths[receiver] == 0), 0, jnp.maximum(slack, 0))
    passed = jax.random.randint(jax.random.fold_in(own, 4), (number_of // 2,), 0, 1 << 20) % (slack + 1)
    lengths = lengths.at[donor].add(-passed).at[receiver].add(passed)
    members = jnp.searchsorted(jnp.cumsum(lengths), jnp.arange(rows * top), side="right").astype(jnp.int32)
    listing = members.reshape(top, rows).T
    listing = listing[jax.random.permutation(jax.random.fold_in(own, 1), rows)]
    turn = jax.random.randint(jax.random.fold_in(own, 2), (rows, 1), 0, top)
    return jnp.take_along_axis(listing, (jnp.arange(top)[None, :] + turn) % top, axis=1)


def shares(amount, total, bound, slope, full):
    portions = [(1 << 20) // math.isqrt(rank ** slope) + 1 for rank in range(1, amount + 1)]
    largest = bound if full else min(bound, max(-(-total // amount), total * portions[0] // sum(portions)))
    least = 1 if total - largest >= amount - 1 else 0
    counts, spare = [largest] + [least] * (amount - 1), total - largest - least * (amount - 1)
    while spare > 0:
        candidates = [i for i in range(1, amount) if counts[i] < largest] or [i for i in range(1, amount) if counts[i] < bound]
        pool, budget = sum([portions[i] for i in candidates]), spare
        for i in candidates:
            extra = min(bound - counts[i], max(1, budget * portions[i] // pool), spare)
            counts[i] = counts[i] + extra
            spare = spare - extra
    return np.array(counts)


def normal_values(key, shape, spread, most, cuts=(), held_as=jnp.bfloat16):
    values = spread * jax.random.normal(key, shape, jnp.float32)
    if cuts:
        values = values * level_of(key, shape, cuts, -0.22, 0.18)
    return jnp.clip(values, -most, most).astype(held_as)


def setup_inputs(seed: int = 0) -> dict:
    key_of = jax.random.split(jax.random.key(seed), 9)
    tokens = normal_values(key_of[0], (TOKENS, D), 1.0, 6.0, ((0, 32),))
    routes_keys = jax.random.split(jax.random.fold_in(key_of[1], 1), TOKENS // TOK_DEV)
    routes_turns = jax.random.permutation(jax.random.fold_in(key_of[1], 3), TOKENS // TOK_DEV)
    routes = jax.vmap(lambda own, number: routed_block(jax.random.fold_in(key_of[1], 2), own, number, TOK_DEV, EXPERTS, 2, CAP, 2))(routes_keys, routes_turns).reshape((TOKENS, 2))
    route_weights = jnp.clip(0.1 + 0.79999997 * jax.random.uniform(key_of[2], (TOKENS, 2), jnp.float32) ** level_of(key_of[2], (TOKENS, 2), ((0, 32),), -0.2, 0.2), 0.1, 0.9)
    placement = jax.random.permutation(key_of[3], EXPERTS).astype(jnp.int32)
    expert_weights = normal_values(key_of[4], (EXPERTS, D, HID), D ** -0.5, 0.09375, ((0, 8), (2, 4)))
    grads = normal_values(key_of[5], (EXPERTS, D, HID), 0.01, 0.059814453, ((0, 8), (2, 4)))
    first_moment = normal_values(key_of[6], (EXPERTS, D, HID), 0.003, 0.017944336, ((0, 8), (2, 4)))
    second_moment = jnp.clip(jnp.exp(math.log(0.0009994507) - 4.609234 * jax.random.uniform(key_of[7], (EXPERTS, D, HID), jnp.float32) ** level_of(key_of[7], (EXPERTS, D, HID), ((0, 8), (2, 4)), -0.2, 0.2)), 9.953975677490234e-06, 0.0009994507).astype(jnp.bfloat16)
    return dict(tokens=tokens, routes=routes, route_weights=route_weights, placement=placement, expert_weights=expert_weights, grads=grads, first_moment=first_moment, second_moment=second_moment)


beta_one = 0.9
beta_two = 0.999
learn_rate = 0.008
adam_eps = 1e-08

def adam_step(weight, gradient, first, second):
    grad_wide = gradient.astype(jnp.float32)
    first_wide = beta_one * first.astype(jnp.float32) + (1.0 - beta_one) * grad_wide
    second_wide = beta_two * second.astype(jnp.float32) + (1.0 - beta_two) * grad_wide * grad_wide
    updated = weight.astype(jnp.float32) - learn_rate * first_wide / (jnp.sqrt(second_wide) + adam_eps)
    return (updated.astype(jnp.bfloat16), first_wide.astype(jnp.bfloat16), second_wide.astype(jnp.bfloat16))

def reference(tokens, routes, route_weights, placement, expert_weights, grads, first_moment, second_moment):
    updated, first_low, second_low = adam_step(expert_weights, grads, first_moment, second_moment)
    new_weights = updated[placement]
    new_first = first_low[placement]
    new_second = second_low[placement]
    blocks = N_DP * N_EXPERT
    entries = routes.reshape(blocks, 2 * TOK_DEV).astype(jnp.int32)
    onehot = (entries[:, :, None] == jnp.arange(EXPERTS, dtype=jnp.int32)[None, None, :]).astype(jnp.int32)
    before = jnp.cumsum(onehot, axis=1) - onehot
    position = lax.optimization_barrier(jnp.sum(before * onehot, axis=2)).astype(jnp.int32)
    slot_index = (jnp.arange(blocks, dtype=jnp.int32)[:, None] * CAP + position).astype(jnp.int32)
    entry_ids = jnp.arange(blocks * 2 * TOK_DEV, dtype=jnp.int32).reshape(blocks, 2 * TOK_DEV)
    table = jnp.zeros((EXPERTS, blocks * CAP), jnp.int32).at[entries, slot_index].set(entry_ids // 2)

    def per_expert(expert_id):
        gathered = tokens[table[expert_id]]
        product = jnp.dot(gathered, updated[expert_id], preferred_element_type=jnp.float32)
        return jax.nn.silu(product).astype(jnp.bfloat16)
    acts = lax.map(per_expert, jnp.arange(EXPERTS, dtype=jnp.int32))
    picked = acts[entries, slot_index].reshape(TOKENS, 2, HID)
    mixed = lax.optimization_barrier(jnp.sum(route_weights[:, :, None] * picked.astype(jnp.float32), axis=1)).astype(jnp.bfloat16)
    return (new_weights, new_first, new_second, mixed)
```

```python
import itertools

import jax
import jax.numpy as jnp
from jax import lax
from jax.sharding import PartitionSpec as P

beta_one = 0.9
beta_two = 0.999
learn_rate = 0.008
adam_eps = 1e-08

CORES = 2


def first_of(gradient, first):
    return beta_one * first.astype(jnp.float32) + (1.0 - beta_one) * gradient.astype(jnp.float32)


def second_of(gradient, second):
    grad_wide = gradient.astype(jnp.float32)
    return beta_two * second.astype(jnp.float32) + (1.0 - beta_two) * grad_wide * grad_wide


def updated_of(weight, gradient, first, second):
    return (
        weight.astype(jnp.float32)
        - learn_rate * first_of(gradient, first) / (jnp.sqrt(second_of(gradient, second)) + adam_eps)
    ).astype(jnp.bfloat16)


def grid_of(experts):
    columns = 1 << ((experts.bit_length() - 1) // 2)
    return experts // columns, columns


def swap(axis, mask, value):
    count = lax.axis_size(axis)
    return lax.ppermute(value, axis, [(i, i ^ mask) for i in range(count)])


def spread(axis, masks, blocks):
    return blocks + [swap(axis, mask, block) for mask in masks for block in blocks]


def pick(index, choices):
    out = choices[0]
    for at, choice in enumerate(choices[1:], 1):
        out = jnp.where(index == at, choice, out)
    return out


def gather_layers(block, layers, columns, z):
    ups, downs = [], []
    up = down = block
    for step in range(1, layers):
        up = lax.ppermute(
            up,
            "expert",
            [(k * columns + x, (k + 1) * columns + x) for k in range(step - 1, layers - 1) for x in range(columns)],
        )
        down = lax.ppermute(
            down,
            "expert",
            [((k + 1) * columns + x, k * columns + x) for k in range(layers - step) for x in range(columns)],
        )
        ups.append(up)
        downs.append(down)
    held = []
    for k in range(layers):
        near = sorted((o for o in range(layers) if o != k), key=lambda o: (abs(o - k), o))
        held.append([k] + near)
    slots = [block]
    for at in range(1, layers):
        groups = {}
        for k in range(layers):
            o = held[k][at]
            key = ("up", k - o) if o < k else ("down", o - k)
            groups.setdefault(key, []).append(k)
        parts = [(ups if key[0] == "up" else downs)[key[1] - 1] for key in groups]
        out = parts[0]
        for part, members in zip(parts[1:], list(groups.values())[1:]):
            here = jnp.zeros((), bool)
            for k in members:
                here = here | (z == k)
            out = jnp.where(here, part, out)
        slots.append(out)
    layer_in = [sum(jnp.where(z == k, held[k][at], 0) for k in range(layers)) for at in range(layers)]
    return slots, layer_in


def at_index(vector, index):
    index = jnp.asarray(index)
    places = jnp.arange(vector.shape[0], dtype=jnp.int32)
    return jnp.sum(jnp.where(index[..., None] == places, vector, 0), axis=-1)


def two_rounds(placement, hosting, layers):
    ids = jnp.arange(2 * layers, dtype=jnp.int32)
    beside = at_index(placement, hosting ^ 1)
    step = at_index(beside, ids ^ 1)
    lowest, reach = ids, ids
    for _ in range(layers - 1):
        reach = at_index(step, reach)
        lowest = jnp.minimum(lowest, reach)
    late = (lowest > at_index(lowest, ids ^ 1)).astype(jnp.int32)
    late_pairs = late.reshape(layers, 2)
    host_pairs = hosting.reshape(layers, 2)
    rounds = []
    for turn in (0, 1):
        column = jnp.where(late_pairs[:, 0] == turn, 0, 1)
        host = jnp.where(column == 0, host_pairs[:, 0], host_pairs[:, 1])
        rounds.append((column, host // 2, host % 2))
    return rounds


def migrate_by_rounds(moments, placement, hosting, layers, z, x):
    perms = list(itertools.permutations(range(layers)))
    table = jnp.array(perms, jnp.int32)

    def branch(perm):
        pairs = [(2 * k + c, 2 * perm[k] + c) for k in range(layers) for c in (0, 1) if perm[k] != k]
        if not pairs:
            return lambda block: block
        return lambda block: lax.ppermute(block, "expert", pairs)

    branches = [branch(perm) for perm in perms]
    rounds = two_rounds(placement, hosting, layers)
    numbers, stays = [], []
    for _, target, _ in rounds:
        match = jnp.all(table == target[None, :], axis=1)
        numbers.append(jnp.sum(jnp.where(match, jnp.arange(len(perms), dtype=jnp.int32), 0)))
        stays.append(at_index(target, z) == z)
    mine_first = at_index(rounds[0][0], z) == x
    arriving = jnp.sum(jnp.where(rounds[0][1] == z, rounds[0][2], 0))
    first_is_mine = arriving == x
    results = []
    for moment in moments:
        rows = moment.shape[0] // 2
        kept = lax.dynamic_slice_in_dim(moment, x * rows, rows, axis=0)
        given = lax.dynamic_slice_in_dim(moment, (1 - x) * rows, rows, axis=0)
        taken = swap("expert", 1, given)
        blocks = (jnp.where(mine_first, kept, taken), jnp.where(mine_first, taken, kept))
        landed = []
        for block, number, stay in zip(blocks, numbers, stays):
            landed.append(jnp.where(stay, block, lax.switch(number, branches, block)))
        own = jnp.where(first_is_mine, landed[0], landed[1])
        other = swap("expert", 1, jnp.where(first_is_mine, landed[1], landed[0]))
        top = jnp.where(x == 0, own, other)
        bottom = jnp.where(x == 0, other, own)
        results.append(jnp.concatenate([top, bottom], axis=0))
    return results


def migrate_by_pieces(moments, placement, experts):
    results = []
    for moment in moments:
        pieces = moment.reshape(experts, moment.shape[0] // experts, moment.shape[1])
        pieces = lax.all_to_all(pieces, "expert", split_axis=0, concat_axis=0, tiled=True)
        pieces = jnp.take(pieces, placement, axis=0)
        pieces = lax.all_to_all(pieces, "expert", split_axis=0, concat_axis=0, tiled=True)
        results.append(pieces.reshape(moment.shape))
    return results


def shards(
    tokens, routes, route_weights, placement, expert_weights, grads, first_moment, second_moment
):
    experts = lax.axis_size("expert")
    layers, columns = grid_of(experts)
    dp_count = lax.axis_size("dp")
    me = lax.axis_index("expert")
    z, x = me // columns, me % columns
    dp_index = lax.axis_index("dp")
    expert_ids = jnp.arange(experts, dtype=jnp.int32)
    tok_count = tokens.shape[0]
    shard = expert_weights.shape[2]

    updated = updated_of(expert_weights[0], grads[0], first_moment[0], second_moment[0])
    first_low = first_of(grads[0], first_moment[0]).astype(jnp.bfloat16)
    second_low = second_of(grads[0], second_moment[0]).astype(jnp.bfloat16)

    hosting = jnp.sum(
        jnp.where(placement[None, :] == expert_ids[:, None], expert_ids[None, :], 0), axis=1
    )

    slots, layer_in = gather_layers(updated, layers, columns, z)

    moments = (first_low, second_low)
    if columns == 2 and layers == 4:
        new_first, new_second = migrate_by_rounds(moments, placement, hosting, layers, z, x)
    else:
        new_first, new_second = migrate_by_pieces(moments, placement, experts)

    def held_block(owner):
        source = at_index(placement, owner)
        slot = sum(jnp.where(layer_in[at] == source // columns, at, 0) for at in range(layers))
        return pick(slot, slots)

    source_column = at_index(placement, me) % columns
    new_weights = held_block(me)
    for mask in range(1, columns):
        came = swap("expert", mask, held_block(me ^ mask))
        new_weights = jnp.where(source_column == (x ^ mask), came, new_weights)

    x_masks = list(range(1, columns))
    y_masks = [CORES * k for k in range(1, dp_count // CORES)]
    named = jnp.sum(
        jnp.where(routes[:, :, None] == expert_ids[None, None, :], route_weights[:, :, None], 0.0), axis=1
    )
    half = tok_count // 2
    upper = spread("expert", x_masks, [tokens[:half]])
    upper = spread("dp", y_masks, upper)
    lower = spread("dp", y_masks, [tokens[half:]])
    lower = spread("expert", x_masks, lower)
    y_count = dp_count // CORES
    lower = [lower[xs * y_count + ys] for ys in range(y_count) for xs in range(columns)]
    near = jnp.concatenate([part for pair in zip(upper, lower) for part in pair], axis=0)
    factors = jnp.concatenate(spread("dp", y_masks, spread("expert", x_masks, [named])), axis=0)

    partial = []
    for rows, scale in ((near, factors), (swap("dp", 1, near), swap("dp", 1, factors))):
        summed = 0.0
        for slot, layer in zip(slots, layer_in):
            act = jax.nn.silu(jnp.dot(rows, slot, preferred_element_type=jnp.float32)).astype(jnp.bfloat16)
            factor = jnp.sum(jnp.where(expert_ids[None, :] == layer * columns + x, scale, 0.0), axis=1)
            summed = summed + factor[:, None] * act.astype(jnp.float32)
        partial.append(summed)
    partial = jnp.concatenate(partial, axis=0)
    partial = partial.reshape(dp_count, columns, tok_count, shard)
    total = partial[:, 0]
    for mask in x_masks:
        total = total + swap("expert", mask, partial[:, mask].astype(jnp.bfloat16)).astype(jnp.float32)
    total = total.astype(jnp.bfloat16)
    pieces = [None] * dp_count
    for core in range(CORES):
        for ys in range(y_count):
            mask = ys * CORES + core
            piece = total[core * y_count + ys]
            pieces[mask] = piece if mask == 0 else swap("dp", mask, piece)
    bit = 1
    while bit < dp_count:
        turned = (dp_index & bit) != 0
        pieces = [jnp.where(turned, pieces[i ^ bit], pieces[i]) for i in range(dp_count)]
        bit *= 2
    mixed = jnp.concatenate(pieces, axis=1)
    return (new_weights[None], new_first[None], new_second[None], mixed)


def solution(mesh):
    return jax.shard_map(
        shards,
        mesh=mesh,
        in_specs=(
            P(("dp", "expert"), None),
            P(("dp", "expert"), None),
            P(("dp", "expert"), None),
            P(),
            P("expert", None, "dp"),
            P("expert", None, "dp"),
            P("expert", None, "dp"),
            P("expert", None, "dp"),
        ),
        out_specs=(
            P("expert", None, "dp"),
            P("expert", None, "dp"),
            P("expert", None, "dp"),
            P(("dp", "expert"), None),
        ),
        check_vma=False,
    )
```

```python
import itertools

import jax
import jax.numpy as jnp
from jax import lax
from jax.experimental import pallas as pl
from jax.experimental.pallas import tpu as pltpu
from jax.sharding import PartitionSpec as P

beta_one = 0.9
beta_two = 0.999
learn_rate = 0.008
adam_eps = 1e-08

CORES = 2


def first_of(gradient, first):
    return beta_one * first.astype(jnp.float32) + (1.0 - beta_one) * gradient.astype(jnp.float32)


def second_of(gradient, second):
    grad_wide = gradient.astype(jnp.float32)
    return beta_two * second.astype(jnp.float32) + (1.0 - beta_two) * grad_wide * grad_wide


def updated_of(weight, gradient, first, second):
    return (
        weight.astype(jnp.float32)
        - learn_rate * first_of(gradient, first) / (jnp.sqrt(second_of(gradient, second)) + adam_eps)
    ).astype(jnp.bfloat16)


def grid_of(experts):
    columns = 1 << ((experts.bit_length() - 1) // 2)
    return experts // columns, columns


def swap(axis, mask, value):
    count = lax.axis_size(axis)
    return lax.ppermute(value, axis, [(i, i ^ mask) for i in range(count)])


def spread(axis, masks, blocks):
    return blocks + [swap(axis, mask, block) for mask in masks for block in blocks]


def pick(index, choices):
    out = choices[0]
    for at, choice in enumerate(choices[1:], 1):
        out = jnp.where(index == at, choice, out)
    return out


def ring_of(layers):
    return list(range(0, layers, 2)) + list(range(1, layers, 2))[::-1]


def ring_step(block, layers, columns):
    ring = ring_of(layers)
    return lax.ppermute(
        block,
        "expert",
        [(k * columns + x, to * columns + x) for k, to in zip(ring, ring[1:] + ring[:1]) for x in range(columns)],
    )


def weighted_products(blocks, weights, scale, prior=None, kept=None):
    count, many = len(blocks), len(weights)
    rows, depth = blocks[0].shape
    wide = weights[0].shape[1]
    steps = count // 2
    pair = 2 * rows
    extra = 0 if prior is None else 1

    def body(*refs):
        sources, held, scales = refs[:count], refs[count : count + many], refs[count + many]
        outs = refs[count + many + 1 + extra : -2]
        window, arrived = refs[-2:]

        def fetch(step, slot):
            for at in range(steps):

                @pl.when(step == at)
                def _():
                    for side in (0, 1):
                        pltpu.make_async_copy(
                            sources[2 * at + side], window.at[slot, pl.ds(side * rows, rows)], arrived.at[slot, side]
                        ).start()

        fetch(0, 0)

        def run(step, carry):
            slot = lax.rem(step, 2)
            fetch(step + 1, 1 - slot)
            for side in (0, 1):
                pltpu.make_async_copy(
                    sources[0], window.at[slot, pl.ds(side * rows, rows)], arrived.at[slot, side]
                ).wait()
            here = pl.ds(pl.multiple_of(step * pair, pair), pair)
            total = refs[count + many + 1][here, :] if extra else jnp.zeros((pair, wide), jnp.float32)
            for at in range(many):
                value = jnp.dot(window[slot], held[at][...], preferred_element_type=jnp.float32)
                act = (value / (1.0 + jnp.exp(-value))).astype(jnp.bfloat16).astype(jnp.float32)
                total = total + scales[here, at : at + 1] * act
            if kept is None:
                outs[0][here, :] = total
            else:

                @pl.when(step < kept // 2)
                def _():
                    outs[0][here, :] = total

                @pl.when(step >= kept // 2)
                def _():
                    there = pl.ds(pl.multiple_of((step - kept // 2) * pair, pair), pair)
                    outs[1][there, :] = total.astype(jnp.bfloat16)

            return carry

        lax.fori_loop(0, steps, run, None)

    near = pl.BlockSpec(memory_space=pltpu.VMEM)
    if kept is None:
        shapes = jax.ShapeDtypeStruct((count * rows, wide), jnp.float32)
    else:
        shapes = (
            jax.ShapeDtypeStruct((kept * rows, wide), jnp.float32),
            jax.ShapeDtypeStruct(((count - kept) * rows, wide), jnp.bfloat16),
        )
    return pl.pallas_call(
        body,
        out_shape=shapes,
        in_specs=[pl.BlockSpec(memory_space=pl.ANY)] * count + [near] * (many + 1 + extra),
        out_specs=near if kept is None else (near, near),
        scratch_shapes=[pltpu.VMEM((2, pair, depth), jnp.bfloat16), pltpu.SemaphoreType.DMA((2, 2))],
        compiler_params=pltpu.CompilerParams(vmem_limit_bytes=40 << 20),
        cost_estimate=pl.CostEstimate(
            flops=2 * count * rows * depth * wide * many,
            bytes_accessed=2 * (count * rows * depth + many * depth * wide),
            transcendentals=count * rows * wide * many,
        ),
    )(*blocks, *weights, scale, *([] if prior is None else [prior]))


def tie(*values):
    return lax.optimization_barrier(values)


def at_index(vector, index):
    index = jnp.asarray(index)
    places = jnp.arange(vector.shape[0], dtype=jnp.int32)
    return jnp.sum(jnp.where(index[..., None] == places, vector, 0), axis=-1)


def two_rounds(placement, hosting, layers):
    ids = jnp.arange(2 * layers, dtype=jnp.int32)
    beside = at_index(placement, hosting ^ 1)
    step = at_index(beside, ids ^ 1)
    lowest, reach = ids, ids
    for _ in range(layers - 1):
        reach = at_index(step, reach)
        lowest = jnp.minimum(lowest, reach)
    late = (lowest > at_index(lowest, ids ^ 1)).astype(jnp.int32)
    late_pairs = late.reshape(layers, 2)
    host_pairs = hosting.reshape(layers, 2)
    rounds = []
    for turn in (0, 1):
        column = jnp.where(late_pairs[:, 0] == turn, 0, 1)
        host = jnp.where(column == 0, host_pairs[:, 0], host_pairs[:, 1])
        rounds.append((column, host // 2, host % 2))
    return rounds


class Rounds:
    def __init__(self, placement, hosting, layers, z, x):
        perms = list(itertools.permutations(range(layers)))
        table = jnp.array(perms, jnp.int32)
        self.x = x
        self.perms = perms
        rounds = two_rounds(placement, hosting, layers)
        numbers, stays = [], []
        for _, target, _ in rounds:
            match = jnp.all(table == target[None, :], axis=1)
            numbers.append(jnp.sum(jnp.where(match, jnp.arange(len(perms), dtype=jnp.int32), 0)))
            stays.append(at_index(target, z) == z)
        mine_first = at_index(rounds[0][0], z) == x
        first_is_mine = jnp.sum(jnp.where(rounds[0][1] == z, rounds[0][2], 0)) == x
        self.plan = (numbers, stays, mine_first, first_is_mine)

    def halves(self, state):
        rows = state.shape[0] // 2
        kept = lax.dynamic_slice_in_dim(state, self.x * rows, rows, axis=0)
        given = lax.dynamic_slice_in_dim(state, (1 - self.x) * rows, rows, axis=0)
        return kept, given

    def blocks(self, kept, taken):
        _, _, mine_first, _ = self.plan
        return jnp.where(mine_first, kept, taken), jnp.where(mine_first, taken, kept)

    def move(self, turn, block, beside=lambda: ()):
        def branch(perm):
            pairs = [(2 * k + c, 2 * to + c) for k, to in enumerate(perm) for c in (0, 1) if to != k]

            def run(block):
                moved = lax.ppermute(block, "expert", pairs) if pairs else block
                return (moved,) + tuple(beside())

            return run

        return lax.switch(self.plan[0][turn], [branch(perm) for perm in self.perms], block)

    def sort(self, blocks, moved):
        _, stays, _, first_is_mine = self.plan
        landed = [jnp.where(stay, block, came) for stay, block, came in zip(stays, blocks, moved)]
        own = jnp.where(first_is_mine, landed[0], landed[1])
        other = jnp.where(first_is_mine, landed[1], landed[0])
        return own, other

    def join(self, own, came):
        top = jnp.where(self.x == 0, own, came)
        bottom = jnp.where(self.x == 0, came, own)
        return jnp.concatenate([top, bottom], axis=0)


def migrate_by_pieces(moments, placement, experts):
    results = []
    for moment in moments:
        pieces = moment.reshape(experts, moment.shape[0] // experts, moment.shape[1])
        pieces = lax.all_to_all(pieces, "expert", split_axis=0, concat_axis=0, tiled=True)
        pieces = jnp.take(pieces, placement, axis=0)
        pieces = lax.all_to_all(pieces, "expert", split_axis=0, concat_axis=0, tiled=True)
        results.append(pieces.reshape(moment.shape))
    return results


def shards(
    tokens, routes, route_weights, placement, expert_weights, grads, first_moment, second_moment
):
    experts = lax.axis_size("expert")
    layers, columns = grid_of(experts)
    dp_count = lax.axis_size("dp")
    me = lax.axis_index("expert")
    z, x = me // columns, me % columns
    dp_index = lax.axis_index("dp")
    expert_ids = jnp.arange(experts, dtype=jnp.int32)
    tok_count = tokens.shape[0]
    shard = expert_weights.shape[2]

    x_masks = list(range(1, columns))
    y_masks = [CORES * k for k in range(1, dp_count // CORES)]
    y_count = dp_count // CORES
    by_rounds = columns == 2 and layers == 4

    hosting = jnp.sum(
        jnp.where(placement[None, :] == expert_ids[:, None], expert_ids[None, :], 0), axis=1
    )
    ring = ring_of(layers)
    layer_in = [
        sum(jnp.where(z == k, ring[(at - back) % layers], 0) for at, k in enumerate(ring)) for back in range(layers)
    ]
    state = (grads[0], first_moment[0], second_moment[0])

    updated = updated_of(expert_weights[0], *state)
    slots = [updated, ring_step(updated, layers, columns)]
    by_x = [swap("expert", mask, tokens) for mask in x_masks]
    by_y = [swap("dp", mask, tokens) for mask in y_masks]
    by_core = swap("dp", 1, tokens)
    named = jnp.sum(
        jnp.where(routes[:, :, None] == expert_ids[None, None, :], route_weights[:, :, None], 0.0), axis=1
    )
    factors = jnp.stack(spread("dp", y_masks, [named]))
    if by_rounds:
        rounds = Rounds(placement, hosting, layers, z, x)
        kept, given = zip(*[rounds.halves(member) for member in state])
        given = jnp.concatenate([first_of(given[0], given[1]), second_of(given[0], given[2])]).astype(jnp.bfloat16)
        kept = jnp.concatenate([first_of(kept[0], kept[1]), second_of(kept[0], kept[2])]).astype(jnp.bfloat16)
        slots, by_x, by_y, by_core, factors, kept, given, rounds.plan = tie(
            slots, by_x, by_y, by_core, factors, kept, given, rounds.plan
        )
    else:
        moments = (first_of(state[0], state[1]).astype(jnp.bfloat16), second_of(state[0], state[2]).astype(jnp.bfloat16))
        new_first, new_second = migrate_by_pieces(moments, placement, experts)

    slots.append(ring_step(slots[1], layers, columns))
    by_xy = [swap("expert", mask, block) for mask in x_masks for block in by_y]
    far = [by_core] + [swap("dp", 1, block) for block in by_y + by_x]
    factors = jnp.stack(spread("expert", x_masks, [factors]))
    if by_rounds:
        slots, by_xy, far, factors, given = tie(slots, by_xy, far, factors, given)

    while len(slots) < layers:
        slots.append(ring_step(slots[-1], layers, columns))
    far = far + [swap("dp", 1, block) for block in by_xy]
    factors = jnp.stack([factors, swap("dp", 1, factors)])
    blocks = []
    for near in ([tokens] + by_y + by_x + by_xy, far):
        mine, others = near[:y_count], near[y_count:]
        by_x_part, by_xy_part = others[: columns - 1], others[columns - 1 :]
        per_x = [mine] + [
            [by_x_part[at]] + by_xy_part[at * (y_count - 1) : (at + 1) * (y_count - 1)] for at in range(columns - 1)
        ]
        blocks.append(per_x)
    blocks = [blocks[core][xs][ys] for xs in range(columns) for core in range(CORES) for ys in range(y_count)]
    factors = factors.transpose(1, 0, 2, 3, 4).reshape(len(blocks) * tok_count, experts)
    scale = jnp.stack(
        [
            jnp.sum(jnp.where(expert_ids[None, :] == layer * columns + x, factors, 0.0), axis=1)
            for layer in layer_in
        ],
        axis=1,
    )
    early = min(3, layers - 1)
    partial = weighted_products(blocks, slots[:early], scale[:, :early])
    if by_rounds:
        taken = swap("expert", 1, given)
        slots, taken, partial, scale, kept = tie(slots, taken, partial, scale, kept)

    def held_block(owner):
        source = at_index(placement, owner)
        slot = sum(jnp.where(layer_in[at] == source // columns, at, 0) for at in range(layers))
        return pick(slot, slots)

    source_column = at_index(placement, me) % columns
    came = [swap("expert", mask, held_block(me ^ mask)) for mask in x_masks]

    def finish():
        return weighted_products(blocks, slots[early:], scale[:, early:], partial, len(blocks) // columns)

    def give(others):
        others = others.reshape(columns - 1, -1, shard)
        return [swap("expert", mask, others[at]) for at, mask in enumerate(x_masks)]

    if by_rounds:
        most = kept.shape[0] * 3 // 4
        first = rounds.blocks(kept[:most], taken[:most])
        second = rounds.blocks(kept[most:], taken[most:])
        total, others = finish()
        first, second, total, others = tie(first, second, total, others)
        (one,) = rounds.move(0, first[0])
        one, first, second, others = tie(one, first, second, others)
        two, *returned = rounds.move(1, first[1], lambda: give(others))
        one, two, returned, total, second, came = tie(one, two, returned, total, second, came)
        most_own, most_other = rounds.sort(first, (one, two))

        most_came = swap("expert", 1, most_other)
        (one,) = rounds.move(0, second[0])
        one, second = tie(one, second)
        (two,) = rounds.move(1, second[1])
        one, two, most_came = tie(one, two, most_came)
        rest_own, rest_other = rounds.sort(second, (one, two))
        rest_came = swap("expert", 1, rest_other)
    else:
        total, others = finish()
        returned = give(others)

    for block in returned:
        total = total + block.astype(jnp.float32)
    total = total.astype(jnp.bfloat16).reshape(CORES, y_count, tok_count, shard)
    pieces = [None] * dp_count
    for core in range(CORES):
        for ys in range(y_count):
            mask = ys * CORES + core
            piece = total[core, ys]
            pieces[mask] = piece if mask == 0 else swap("dp", mask, piece)
    new_weights = held_block(me)
    for mask, block in zip(x_masks, came):
        new_weights = jnp.where(source_column == (x ^ mask), block, new_weights)
    bit = 1
    while bit < dp_count:
        turned = (dp_index & bit) != 0
        pieces = [jnp.where(turned, pieces[i ^ bit], pieces[i]) for i in range(dp_count)]
        bit *= 2
    mixed = jnp.concatenate(pieces, axis=1)
    if by_rounds:
        half = most_own.shape[0] * 2 // 3
        new_first = rounds.join(most_own[:half], most_came[:half])
        new_second = rounds.join(
            jnp.concatenate([most_own[half:], rest_own]), jnp.concatenate([most_came[half:], rest_came])
        )
    return (new_weights[None], new_first[None], new_second[None], mixed)


def solution(mesh):
    return jax.shard_map(
        shards,
        mesh=mesh,
        in_specs=(
            P(("dp", "expert"), None),
            P(("dp", "expert"), None),
            P(("dp", "expert"), None),
            P(),
            P("expert", None, "dp"),
            P("expert", None, "dp"),
            P("expert", None, "dp"),
            P("expert", None, "dp"),
        ),
        out_specs=(
            P("expert", None, "dp"),
            P("expert", None, "dp"),
            P("expert", None, "dp"),
            P(("dp", "expert"), None),
        ),
        check_vma=False,
    )
```

```python
import itertools

import jax
import jax.numpy as jnp
from jax import lax
from jax.experimental import pallas as pl
from jax.experimental.pallas import tpu as pltpu
from jax.sharding import PartitionSpec as P

beta_one = 0.9
beta_two = 0.999
learn_rate = 0.008
adam_eps = 1e-08

CORES = 2


def first_of(gradient, first):
    return beta_one * first.astype(jnp.float32) + (1.0 - beta_one) * gradient.astype(jnp.float32)


def second_of(gradient, second):
    grad_wide = gradient.astype(jnp.float32)
    return beta_two * second.astype(jnp.float32) + (1.0 - beta_two) * grad_wide * grad_wide


def updated_of(weight, gradient, first, second):
    return (
        weight.astype(jnp.float32)
        - learn_rate * first_of(gradient, first) / (jnp.sqrt(second_of(gradient, second)) + adam_eps)
    ).astype(jnp.bfloat16)


def grid_of(experts):
    columns = 1 << ((experts.bit_length() - 1) // 2)
    return experts // columns, columns


def swap(axis, mask, value):
    count = lax.axis_size(axis)
    return lax.ppermute(value, axis, [(i, i ^ mask) for i in range(count)])


def spread(axis, masks, blocks):
    return blocks + [swap(axis, mask, block) for mask in masks for block in blocks]


def pick(index, choices):
    out = choices[0]
    for at, choice in enumerate(choices[1:], 1):
        out = jnp.where(index == at, choice, out)
    return out


def ring_of(layers):
    return list(range(0, layers, 2)) + list(range(1, layers, 2))[::-1]


def ring_step(block, layers, columns):
    ring = ring_of(layers)
    return lax.ppermute(
        block,
        "expert",
        [(k * columns + x, to * columns + x) for k, to in zip(ring, ring[1:] + ring[:1]) for x in range(columns)],
    )


def weighted_products(blocks, weights, scale, prior=None, kept=None):
    count, many = len(blocks), len(weights)
    rows, depth = blocks[0].shape
    wide = weights[0].shape[1]
    steps = count // 2
    pair = 2 * rows
    extra = 0 if prior is None else 1

    def body(*refs):
        sources, held, scales = refs[:count], refs[count : count + many], refs[count + many]
        outs = refs[count + many + 1 + extra : -2]
        window, arrived = refs[-2:]

        def fetch(step, slot):
            for at in range(steps):

                @pl.when(step == at)
                def _():
                    for side in (0, 1):
                        pltpu.make_async_copy(
                            sources[2 * at + side], window.at[slot, pl.ds(side * rows, rows)], arrived.at[slot, side]
                        ).start()

        fetch(0, 0)

        def run(step, carry):
            slot = lax.rem(step, 2)
            fetch(step + 1, 1 - slot)
            for side in (0, 1):
                pltpu.make_async_copy(
                    sources[0], window.at[slot, pl.ds(side * rows, rows)], arrived.at[slot, side]
                ).wait()
            here = pl.ds(pl.multiple_of(step * pair, pair), pair)
            total = refs[count + many + 1][here, :] if extra else jnp.zeros((pair, wide), jnp.float32)
            for at in range(many):
                value = jnp.dot(window[slot], held[at][...], preferred_element_type=jnp.float32)
                act = (value / (1.0 + jnp.exp(-value))).astype(jnp.bfloat16).astype(jnp.float32)
                total = total + scales[here, at : at + 1] * act
            if kept is None:
                outs[0][here, :] = total
            else:

                @pl.when(step < kept // 2)
                def _():
                    outs[0][here, :] = total

                @pl.when(step >= kept // 2)
                def _():
                    there = pl.ds(pl.multiple_of((step - kept // 2) * pair, pair), pair)
                    outs[1][there, :] = total.astype(jnp.bfloat16)

            return carry

        lax.fori_loop(0, steps, run, None)

    near = pl.BlockSpec(memory_space=pltpu.VMEM)
    if kept is None:
        shapes = jax.ShapeDtypeStruct((count * rows, wide), jnp.float32)
    else:
        shapes = (
            jax.ShapeDtypeStruct((kept * rows, wide), jnp.float32),
            jax.ShapeDtypeStruct(((count - kept) * rows, wide), jnp.bfloat16),
        )
    return pl.pallas_call(
        body,
        out_shape=shapes,
        in_specs=[pl.BlockSpec(memory_space=pl.ANY)] * count + [near] * (many + 1 + extra),
        out_specs=near if kept is None else (near, near),
        scratch_shapes=[pltpu.VMEM((2, pair, depth), jnp.bfloat16), pltpu.SemaphoreType.DMA((2, 2))],
        compiler_params=pltpu.CompilerParams(vmem_limit_bytes=60 << 20),
        cost_estimate=pl.CostEstimate(
            flops=2 * count * rows * depth * wide * many,
            bytes_accessed=2 * (count * rows * depth + many * depth * wide),
            transcendentals=count * rows * wide * many,
        ),
    )(*blocks, *weights, scale, *([] if prior is None else [prior]))


def tie(*values):
    return lax.optimization_barrier(values)


def at_index(vector, index):
    index = jnp.asarray(index)
    places = jnp.arange(vector.shape[0], dtype=jnp.int32)
    return jnp.sum(jnp.where(index[..., None] == places, vector, 0), axis=-1)


def two_rounds(placement, hosting, layers):
    ids = jnp.arange(2 * layers, dtype=jnp.int32)
    beside = at_index(placement, hosting ^ 1)
    step = at_index(beside, ids ^ 1)
    lowest, reach = ids, ids
    for _ in range(layers - 1):
        reach = at_index(step, reach)
        lowest = jnp.minimum(lowest, reach)
    late = (lowest > at_index(lowest, ids ^ 1)).astype(jnp.int32)
    late_pairs = late.reshape(layers, 2)
    host_pairs = hosting.reshape(layers, 2)
    rounds = []
    for turn in (0, 1):
        column = jnp.where(late_pairs[:, 0] == turn, 0, 1)
        host = jnp.where(column == 0, host_pairs[:, 0], host_pairs[:, 1])
        rounds.append((column, host // 2, host % 2))
    return rounds


class Rounds:
    def __init__(self, placement, hosting, layers, z, x):
        perms = list(itertools.permutations(range(layers)))
        table = jnp.array(perms, jnp.int32)
        self.x = x
        self.perms = perms
        rounds = two_rounds(placement, hosting, layers)
        numbers, stays = [], []
        for _, target, _ in rounds:
            match = jnp.all(table == target[None, :], axis=1)
            numbers.append(jnp.sum(jnp.where(match, jnp.arange(len(perms), dtype=jnp.int32), 0)))
            stays.append(at_index(target, z) == z)
        mine_first = at_index(rounds[0][0], z) == x
        first_is_mine = jnp.sum(jnp.where(rounds[0][1] == z, rounds[0][2], 0)) == x
        self.plan = (numbers, stays, mine_first, first_is_mine)

    def halves(self, state):
        rows = state.shape[0] // 2
        kept = lax.dynamic_slice_in_dim(state, self.x * rows, rows, axis=0)
        given = lax.dynamic_slice_in_dim(state, (1 - self.x) * rows, rows, axis=0)
        return kept, given

    def blocks(self, kept, taken):
        _, _, mine_first, _ = self.plan
        return jnp.where(mine_first, kept, taken), jnp.where(mine_first, taken, kept)

    def move(self, turn, block, beside=lambda: ()):
        def branch(perm):
            pairs = [(2 * k + c, 2 * to + c) for k, to in enumerate(perm) for c in (0, 1) if to != k]

            def run(block):
                moved = lax.ppermute(block, "expert", pairs) if pairs else block
                return (moved,) + tuple(beside())

            return run

        return lax.switch(self.plan[0][turn], [branch(perm) for perm in self.perms], block)

    def sort(self, blocks, moved):
        _, stays, _, first_is_mine = self.plan
        landed = [jnp.where(stay, block, came) for stay, block, came in zip(stays, blocks, moved)]
        own = jnp.where(first_is_mine, landed[0], landed[1])
        other = jnp.where(first_is_mine, landed[1], landed[0])
        return own, other

    def join(self, own, came):
        top = jnp.where(self.x == 0, own, came)
        bottom = jnp.where(self.x == 0, came, own)
        return jnp.concatenate([top, bottom], axis=0)


def migrate_by_pieces(moments, placement, experts):
    results = []
    for moment in moments:
        pieces = moment.reshape(experts, moment.shape[0] // experts, moment.shape[1])
        pieces = lax.all_to_all(pieces, "expert", split_axis=0, concat_axis=0, tiled=True)
        pieces = jnp.take(pieces, placement, axis=0)
        pieces = lax.all_to_all(pieces, "expert", split_axis=0, concat_axis=0, tiled=True)
        results.append(pieces.reshape(moment.shape))
    return results


def shards(
    tokens, routes, route_weights, placement, expert_weights, grads, first_moment, second_moment
):
    experts = lax.axis_size("expert")
    layers, columns = grid_of(experts)
    dp_count = lax.axis_size("dp")
    me = lax.axis_index("expert")
    z, x = me // columns, me % columns
    dp_index = lax.axis_index("dp")
    expert_ids = jnp.arange(experts, dtype=jnp.int32)
    tok_count = tokens.shape[0]
    shard = expert_weights.shape[2]

    x_masks = list(range(1, columns))
    y_masks = [CORES * k for k in range(1, dp_count // CORES)]
    y_count = dp_count // CORES
    by_rounds = columns == 2 and layers == 4

    hosting = jnp.sum(
        jnp.where(placement[None, :] == expert_ids[:, None], expert_ids[None, :], 0), axis=1
    )
    ring = ring_of(layers)
    layer_in = [
        sum(jnp.where(z == k, ring[(at - back) % layers], 0) for at, k in enumerate(ring)) for back in range(layers)
    ]
    state = (grads[0], first_moment[0], second_moment[0])

    updated = updated_of(expert_weights[0], *state)
    slots = [updated, ring_step(updated, layers, columns)]
    if by_rounds:
        updated, tokens = tie(updated, tokens)
    by_x = [swap("expert", mask, tokens) for mask in x_masks]
    by_y = [swap("dp", mask, tokens) for mask in y_masks]
    by_core = swap("dp", 1, tokens)
    named = jnp.sum(
        jnp.where(routes[:, :, None] == expert_ids[None, None, :], route_weights[:, :, None], 0.0), axis=1
    )
    factors = jnp.stack(spread("dp", y_masks, [named]))
    sources = [at_index(placement, me ^ mask) for mask in range(columns)]
    source_slots = [
        sum(jnp.where(layer_in[at] == source // columns, at, 0) for at in range(layers)) for source in sources
    ]
    came_from = sources[0] % columns ^ x
    if by_rounds:
        rounds = Rounds(placement, hosting, layers, z, x)
        kept, given = zip(*[rounds.halves(member) for member in state])
        given = jnp.concatenate([first_of(given[0], given[1]), second_of(given[0], given[2])]).astype(jnp.bfloat16)
        kept = jnp.concatenate([first_of(kept[0], kept[1]), second_of(kept[0], kept[2])]).astype(jnp.bfloat16)
        slots, by_x, by_y, by_core, factors, kept, given, rounds.plan, source_slots, came_from = tie(
            slots, by_x, by_y, by_core, factors, kept, given, rounds.plan, source_slots, came_from
        )
    else:
        moments = (first_of(state[0], state[1]).astype(jnp.bfloat16), second_of(state[0], state[2]).astype(jnp.bfloat16))
        new_first, new_second = migrate_by_pieces(moments, placement, experts)

    slots.append(ring_step(slots[1], layers, columns))
    by_xy = [swap("dp", mask, block) for block in by_x for mask in y_masks]
    far = [by_core] + [swap("dp", 1, block) for block in by_y + by_x]
    factors = jnp.stack(spread("expert", x_masks, [factors]))
    if by_rounds:
        taken = swap("expert", 1, given)
        slots, by_xy, far, factors, taken = tie(slots, by_xy, far, factors, taken)

    while len(slots) < layers:
        slots.append(ring_step(slots[-1], layers, columns))
    far = far + [swap("dp", 1, block) for block in by_xy]
    factors = jnp.stack([factors, swap("dp", 1, factors)])
    blocks = []
    for near in ([tokens] + by_y + by_x + by_xy, far):
        mine, others = near[:y_count], near[y_count:]
        by_x_part, by_xy_part = others[: columns - 1], others[columns - 1 :]
        per_x = [mine] + [
            [by_x_part[at]] + by_xy_part[at * (y_count - 1) : (at + 1) * (y_count - 1)] for at in range(columns - 1)
        ]
        blocks.append(per_x)
    blocks = [blocks[core][xs][ys] for xs in range(columns) for core in range(CORES) for ys in range(y_count)]
    factors = factors.transpose(1, 0, 2, 3, 4).reshape(len(blocks) * tok_count, experts)
    scale = jnp.stack(
        [
            jnp.sum(jnp.where(expert_ids[None, :] == layer * columns + x, factors, 0.0), axis=1)
            for layer in layer_in
        ],
        axis=1,
    )
    early = min(3, layers - 1)
    partial = weighted_products(blocks, slots[:early], scale[:, :early])
    scale = scale[:, early:]
    if by_rounds:
        most = kept.shape[0] * 11 // 16
        first = rounds.blocks(kept[:most], taken[:most])
        second = rounds.blocks(kept[most:], taken[most:])
        slots, first, second, partial, scale = tie(slots, first, second, partial, scale)

    came = [swap("expert", mask, pick(source_slots[mask], slots)) for mask in x_masks]

    def finish():
        return weighted_products(blocks, slots[early:], scale, partial, len(blocks) // columns)

    def give(others):
        others = others.reshape(columns - 1, -1, shard)
        return [swap("expert", mask, others[at]) for at, mask in enumerate(x_masks)]

    if by_rounds:
        total, others = finish()
        first, second, total, others = tie(first, second, total, others)
        (one,) = rounds.move(0, first[0])
        one, first, second, others = tie(one, first, second, others)
        two, *returned = rounds.move(1, first[1], lambda: give(others))
        one, two, second, came = tie(one, two, second, came)
        most_own, most_other = rounds.sort(first, (one, two))

        most_came = swap("expert", 1, most_other)
        (one,) = rounds.move(0, second[0])
        one, second = tie(one, second)
        (two,) = rounds.move(1, second[1])
        one, two, returned, total = tie(one, two, returned, total)
        rest_own, rest_other = rounds.sort(second, (one, two))
        rest_came = swap("expert", 1, rest_other)
    else:
        total, others = finish()
        returned = give(others)

    for block in returned:
        total = total + block.astype(jnp.float32)
    total = total.astype(jnp.bfloat16).reshape(CORES, y_count, tok_count, shard)
    pieces = [None] * dp_count
    for core in range(CORES):
        for ys in range(y_count):
            mask = ys * CORES + core
            piece = total[core, ys]
            pieces[mask] = piece if mask == 0 else swap("dp", mask, piece)
    new_weights = pick(source_slots[0], slots)
    for mask, block in zip(x_masks, came):
        new_weights = jnp.where(came_from == mask, block, new_weights)
    bit = 1
    while bit < dp_count:
        turned = (dp_index & bit) != 0
        pieces = [jnp.where(turned, pieces[i ^ bit], pieces[i]) for i in range(dp_count)]
        bit *= 2
    mixed = jnp.concatenate(pieces, axis=1)
    if by_rounds:
        half = kept.shape[0] // 2
        new_first = rounds.join(most_own[:half], most_came[:half])
        new_second = rounds.join(
            jnp.concatenate([most_own[half:], rest_own]), jnp.concatenate([most_came[half:], rest_came])
        )
    return (new_weights[None], new_first[None], new_second[None], mixed)


def solution(mesh):
    return jax.shard_map(
        shards,
        mesh=mesh,
        in_specs=(
            P(("dp", "expert"), None),
            P(("dp", "expert"), None),
            P(("dp", "expert"), None),
            P(),
            P("expert", None, "dp"),
            P("expert", None, "dp"),
            P("expert", None, "dp"),
            P("expert", None, "dp"),
        ),
        out_specs=(
            P("expert", None, "dp"),
            P("expert", None, "dp"),
            P("expert", None, "dp"),
            P(("dp", "expert"), None),
        ),
        check_vma=False,
    )
```

```python
import itertools

import jax
import jax.numpy as jnp
from jax import lax
from jax.experimental import pallas as pl
from jax.experimental.pallas import tpu as pltpu
from jax.sharding import PartitionSpec as P

beta_one = 0.9
beta_two = 0.999
learn_rate = 0.008
adam_eps = 1e-08

CORES = 2


def first_of(gradient, first):
    return beta_one * first.astype(jnp.float32) + (1.0 - beta_one) * gradient.astype(jnp.float32)


def second_of(gradient, second):
    grad_wide = gradient.astype(jnp.float32)
    return beta_two * second.astype(jnp.float32) + (1.0 - beta_two) * grad_wide * grad_wide


def updated_of(weight, gradient, first, second):
    return (
        weight.astype(jnp.float32)
        - learn_rate * first_of(gradient, first) / (jnp.sqrt(second_of(gradient, second)) + adam_eps)
    ).astype(jnp.bfloat16)


def grid_of(experts):
    columns = 1 << ((experts.bit_length() - 1) // 2)
    return experts // columns, columns


def swap(axis, mask, value):
    count = lax.axis_size(axis)
    return lax.ppermute(value, axis, [(i, i ^ mask) for i in range(count)])


def spread(axis, masks, blocks):
    return blocks + [swap(axis, mask, block) for mask in masks for block in blocks]


def pick(index, choices):
    out = choices[0]
    for at, choice in enumerate(choices[1:], 1):
        out = jnp.where(index == at, choice, out)
    return out


def ring_of(layers):
    return list(range(0, layers, 2)) + list(range(1, layers, 2))[::-1]


def ring_step(block, layers, columns):
    ring = ring_of(layers)
    return lax.ppermute(
        block,
        "expert",
        [(k * columns + x, to * columns + x) for k, to in zip(ring, ring[1:] + ring[:1]) for x in range(columns)],
    )


def weighted_products(blocks, weights, scale, prior=None, kept=None):
    count, many = len(blocks), len(weights)
    rows, depth = blocks[0].shape
    wide = weights[0].shape[1]
    steps = count // 2
    pair = 2 * rows
    extra = 0 if prior is None else 1

    def body(*refs):
        sources, held, scales = refs[:count], refs[count : count + many], refs[count + many]
        outs = refs[count + many + 1 + extra : -2]
        window, arrived = refs[-2:]

        def fetch(step, slot):
            for at in range(steps):

                @pl.when(step == at)
                def _():
                    for side in (0, 1):
                        pltpu.make_async_copy(
                            sources[2 * at + side], window.at[slot, pl.ds(side * rows, rows)], arrived.at[slot, side]
                        ).start()

        fetch(0, 0)

        def run(step, carry):
            slot = lax.rem(step, 2)
            fetch(step + 1, 1 - slot)
            for side in (0, 1):
                pltpu.make_async_copy(
                    sources[0], window.at[slot, pl.ds(side * rows, rows)], arrived.at[slot, side]
                ).wait()
            here = pl.ds(pl.multiple_of(step * pair, pair), pair)
            total = refs[count + many + 1][here, :] if extra else jnp.zeros((pair, wide), jnp.float32)
            for at in range(many):
                value = jnp.dot(window[slot], held[at][...], preferred_element_type=jnp.float32)
                act = (value / (1.0 + jnp.exp(-value))).astype(jnp.bfloat16).astype(jnp.float32)
                total = total + scales[here, at : at + 1] * act
            if kept is None:
                outs[0][here, :] = total
            else:

                @pl.when(step < kept // 2)
                def _():
                    outs[0][here, :] = total

                @pl.when(step >= kept // 2)
                def _():
                    there = pl.ds(pl.multiple_of((step - kept // 2) * pair, pair), pair)
                    outs[1][there, :] = total.astype(jnp.bfloat16)

            return carry

        lax.fori_loop(0, steps, run, None)

    near = pl.BlockSpec(memory_space=pltpu.VMEM)
    if kept is None:
        shapes = jax.ShapeDtypeStruct((count * rows, wide), jnp.float32)
    else:
        shapes = (
            jax.ShapeDtypeStruct((kept * rows, wide), jnp.float32),
            jax.ShapeDtypeStruct(((count - kept) * rows, wide), jnp.bfloat16),
        )
    return pl.pallas_call(
        body,
        out_shape=shapes,
        in_specs=[pl.BlockSpec(memory_space=pl.ANY)] * count + [near] * (many + 1 + extra),
        out_specs=near if kept is None else (near, near),
        scratch_shapes=[pltpu.VMEM((2, pair, depth), jnp.bfloat16), pltpu.SemaphoreType.DMA((2, 2))],
        compiler_params=pltpu.CompilerParams(vmem_limit_bytes=60 << 20),
        cost_estimate=pl.CostEstimate(
            flops=2 * count * rows * depth * wide * many,
            bytes_accessed=2 * (count * rows * depth + many * depth * wide),
            transcendentals=count * rows * wide * many,
        ),
    )(*blocks, *weights, scale, *([] if prior is None else [prior]))


def tie(*values):
    return lax.optimization_barrier(values)


def at_index(vector, index):
    index = jnp.asarray(index)
    places = jnp.arange(vector.shape[0], dtype=jnp.int32)
    return jnp.sum(jnp.where(index[..., None] == places, vector, 0), axis=-1)


def two_rounds(placement, hosting, layers):
    ids = jnp.arange(2 * layers, dtype=jnp.int32)
    beside = at_index(placement, hosting ^ 1)
    step = at_index(beside, ids ^ 1)
    lowest, reach = ids, ids
    for _ in range(layers - 1):
        reach = at_index(step, reach)
        lowest = jnp.minimum(lowest, reach)
    late = (lowest > at_index(lowest, ids ^ 1)).astype(jnp.int32)
    late_pairs = late.reshape(layers, 2)
    host_pairs = hosting.reshape(layers, 2)
    rounds = []
    for turn in (0, 1):
        column = jnp.where(late_pairs[:, 0] == turn, 0, 1)
        host = jnp.where(column == 0, host_pairs[:, 0], host_pairs[:, 1])
        rounds.append((column, host // 2, host % 2))
    return rounds


class Rounds:
    def __init__(self, placement, hosting, layers, z, x):
        perms = list(itertools.permutations(range(layers)))
        table = jnp.array(perms, jnp.int32)
        self.x = x
        self.perms = perms
        rounds = two_rounds(placement, hosting, layers)
        numbers, stays = [], []
        for _, target, _ in rounds:
            match = jnp.all(table == target[None, :], axis=1)
            numbers.append(jnp.sum(jnp.where(match, jnp.arange(len(perms), dtype=jnp.int32), 0)))
            stays.append(at_index(target, z) == z)
        mine_first = at_index(rounds[0][0], z) == x
        first_is_mine = jnp.sum(jnp.where(rounds[0][1] == z, rounds[0][2], 0)) == x
        self.plan = (numbers, stays, mine_first, first_is_mine)

    def halves(self, state):
        rows = state.shape[0] // 2
        kept = lax.dynamic_slice_in_dim(state, self.x * rows, rows, axis=0)
        given = lax.dynamic_slice_in_dim(state, (1 - self.x) * rows, rows, axis=0)
        return kept, given

    def blocks(self, kept, taken):
        _, _, mine_first, _ = self.plan
        return jnp.where(mine_first, kept, taken), jnp.where(mine_first, taken, kept)

    def move(self, turn, block, beside=lambda: ()):
        def branch(perm):
            pairs = [(2 * k + c, 2 * to + c) for k, to in enumerate(perm) for c in (0, 1) if to != k]

            def run(block):
                moved = lax.ppermute(block, "expert", pairs) if pairs else block
                return (moved,) + tuple(beside())

            return run

        return lax.switch(self.plan[0][turn], [branch(perm) for perm in self.perms], block)

    def pass_on(self, blocks, moved):
        _, stays, _, first_is_mine = self.plan
        landed = [jnp.where(stay, block, came) for stay, block, came in zip(stays, blocks, moved)]
        other = jnp.where(first_is_mine, landed[1], landed[0])
        other, blocks, moved = tie(other, blocks, moved)
        landed = [jnp.where(stay, block, came) for stay, block, came in zip(stays, blocks, moved)]
        return jnp.where(first_is_mine, landed[0], landed[1]), other

    def join(self, own, came):
        top = jnp.where(self.x == 0, own, came)
        bottom = jnp.where(self.x == 0, came, own)
        return jnp.concatenate([top, bottom], axis=0)


def migrate_by_pieces(moments, placement, experts):
    results = []
    for moment in moments:
        pieces = moment.reshape(experts, moment.shape[0] // experts, moment.shape[1])
        pieces = lax.all_to_all(pieces, "expert", split_axis=0, concat_axis=0, tiled=True)
        pieces = jnp.take(pieces, placement, axis=0)
        pieces = lax.all_to_all(pieces, "expert", split_axis=0, concat_axis=0, tiled=True)
        results.append(pieces.reshape(moment.shape))
    return results


def shards(
    tokens, routes, route_weights, placement, expert_weights, grads, first_moment, second_moment
):
    experts = lax.axis_size("expert")
    layers, columns = grid_of(experts)
    dp_count = lax.axis_size("dp")
    me = lax.axis_index("expert")
    z, x = me // columns, me % columns
    dp_index = lax.axis_index("dp")
    expert_ids = jnp.arange(experts, dtype=jnp.int32)
    tok_count = tokens.shape[0]
    shard = expert_weights.shape[2]

    x_masks = list(range(1, columns))
    y_masks = [CORES * k for k in range(1, dp_count // CORES)]
    y_count = dp_count // CORES
    by_rounds = columns == 2 and layers == 4

    hosting = jnp.sum(
        jnp.where(placement[None, :] == expert_ids[:, None], expert_ids[None, :], 0), axis=1
    )
    ring = ring_of(layers)
    layer_in = [
        sum(jnp.where(z == k, ring[(at - back) % layers], 0) for at, k in enumerate(ring)) for back in range(layers)
    ]
    state = (grads[0], first_moment[0], second_moment[0])

    updated = updated_of(expert_weights[0], *state)
    slots = [updated, ring_step(updated, layers, columns)]
    if by_rounds:
        updated, tokens = tie(updated, tokens)
    by_x = [swap("expert", mask, tokens) for mask in x_masks]
    by_y = [swap("dp", mask, tokens) for mask in y_masks]
    by_core = swap("dp", 1, tokens)
    named = jnp.sum(
        jnp.where(routes[:, :, None] == expert_ids[None, None, :], route_weights[:, :, None], 0.0), axis=1
    )
    factors = jnp.stack(spread("dp", [1], [named]))
    sources = [at_index(placement, me ^ mask) for mask in range(columns)]
    source_slots = [
        sum(jnp.where(layer_in[at] == source // columns, at, 0) for at in range(layers)) for source in sources
    ]
    came_from = sources[0] % columns ^ x
    if by_rounds:
        rounds = Rounds(placement, hosting, layers, z, x)
        kept, given = zip(*[rounds.halves(member) for member in state])
        given = jnp.concatenate([first_of(given[0], given[1]), second_of(given[0], given[2])]).astype(jnp.bfloat16)
        kept = jnp.concatenate([first_of(kept[0], kept[1]), second_of(kept[0], kept[2])]).astype(jnp.bfloat16)
        slots, factors, kept, given, rounds.plan, source_slots, came_from = tie(
            slots, factors, kept, given, rounds.plan, source_slots, came_from
        )
    else:
        moments = (first_of(state[0], state[1]).astype(jnp.bfloat16), second_of(state[0], state[2]).astype(jnp.bfloat16))
        new_first, new_second = migrate_by_pieces(moments, placement, experts)

    slots.append(ring_step(slots[1], layers, columns))
    by_xy = [swap("dp", mask, block) for block in by_x for mask in y_masks]
    far = [by_core] + [swap("dp", 1, block) for block in by_y + by_x]
    factors = jnp.stack(spread("dp", y_masks, [factors]))
    if by_rounds:
        taken = swap("expert", 1, given)
        slots, by_xy, far, factors, taken = tie(slots, by_xy, far, factors, taken)

    while len(slots) < layers:
        slots.append(ring_step(slots[-1], layers, columns))
    far = far + [swap("dp", 1, block) for block in by_xy]
    factors = jnp.stack(spread("expert", x_masks, [factors]))
    blocks = []
    for near in ([tokens] + by_y + by_x + by_xy, far):
        mine, others = near[:y_count], near[y_count:]
        by_x_part, by_xy_part = others[: columns - 1], others[columns - 1 :]
        per_x = [mine] + [
            [by_x_part[at]] + by_xy_part[at * (y_count - 1) : (at + 1) * (y_count - 1)] for at in range(columns - 1)
        ]
        blocks.append(per_x)
    blocks = [blocks[core][xs][ys] for xs in range(columns) for core in range(CORES) for ys in range(y_count)]
    factors = factors.transpose(0, 2, 1, 3, 4).reshape(len(blocks) * tok_count, experts)
    scale = jnp.stack(
        [
            jnp.sum(jnp.where(expert_ids[None, :] == layer * columns + x, factors, 0.0), axis=1)
            for layer in layer_in
        ],
        axis=1,
    )
    early = min(3, layers - 1)
    partial = weighted_products(blocks, slots[:early], scale[:, :early])
    scale = scale[:, early:]
    found = [pick(number, slots[:early]) for number in source_slots]
    if by_rounds:
        most = kept.shape[0] * 3 // 4
        first = rounds.blocks(kept[:most], taken[:most])
        second = rounds.blocks(kept[most:], taken[most:])
        slots, first, second, partial, scale, found = tie(slots, first, second, partial, scale, found)

    def needed(mask):
        out = found[mask]
        for at in range(early, layers):
            out = jnp.where(source_slots[mask] == at, slots[at], out)
        return out

    came = [swap("expert", mask, needed(mask)) for mask in x_masks]

    def finish():
        return weighted_products(blocks, slots[early:], scale, partial, len(blocks) // columns)

    def give(others):
        others = others.reshape(columns - 1, -1, shard)
        return [swap("expert", mask, others[at]) for at, mask in enumerate(x_masks)]

    if by_rounds:
        total, others = finish()
        first, second, total, others = tie(first, second, total, others)
        (one,) = rounds.move(0, first[0])
        one, first, second, others = tie(one, first, second, others)
        two, *returned = rounds.move(1, first[1], lambda: give(others))
        one, two, second, came = tie(one, two, second, came)
        most_own, most_other = rounds.pass_on(first, (one, two))

        most_came = swap("expert", 1, most_other)
        (one,) = rounds.move(0, second[0])
        one, second = tie(one, second)
        (two,) = rounds.move(1, second[1])
        one, two, returned, total = tie(one, two, returned, total)
        rest_own, rest_other = rounds.pass_on(second, (one, two))
        rest_came = swap("expert", 1, rest_other)
    else:
        total, others = finish()
        returned = give(others)

    for block in returned:
        total = total + block.astype(jnp.float32)
    total = total.astype(jnp.bfloat16).reshape(CORES, y_count, tok_count, shard)
    pieces = [None] * dp_count
    for core in range(CORES):
        for ys in range(y_count):
            mask = ys * CORES + core
            piece = total[core, ys]
            pieces[mask] = piece if mask == 0 else swap("dp", mask, piece)
    new_weights = needed(0)
    for mask, block in zip(x_masks, came):
        new_weights = jnp.where(came_from == mask, block, new_weights)
    bit = 1
    while bit < dp_count:
        turned = (dp_index & bit) != 0
        pieces = [jnp.where(turned, pieces[i ^ bit], pieces[i]) for i in range(dp_count)]
        bit *= 2
    mixed = jnp.concatenate(pieces, axis=1)
    if by_rounds:
        half = kept.shape[0] // 2
        new_first = rounds.join(most_own[:half], most_came[:half])
        new_second = rounds.join(
            jnp.concatenate([most_own[half:], rest_own]), jnp.concatenate([most_came[half:], rest_came])
        )
    return (new_weights[None], new_first[None], new_second[None], mixed)


def solution(mesh):
    return jax.shard_map(
        shards,
        mesh=mesh,
        in_specs=(
            P(("dp", "expert"), None),
            P(("dp", "expert"), None),
            P(("dp", "expert"), None),
            P(),
            P("expert", None, "dp"),
            P("expert", None, "dp"),
            P("expert", None, "dp"),
            P("expert", None, "dp"),
        ),
        out_specs=(
            P("expert", None, "dp"),
            P("expert", None, "dp"),
            P("expert", None, "dp"),
            P(("dp", "expert"), None),
        ),
        check_vma=False,
    )
```

```python
import itertools

import jax
import jax.numpy as jnp
from jax import lax
from jax.experimental import pallas as pl
from jax.experimental.pallas import tpu as pltpu
from jax.sharding import PartitionSpec as P

beta_one = 0.9
beta_two = 0.999
learn_rate = 0.008
adam_eps = 1e-08

CORES = 2


def first_of(gradient, first):
    return beta_one * first.astype(jnp.float32) + (1.0 - beta_one) * gradient.astype(jnp.float32)


def second_of(gradient, second):
    grad_wide = gradient.astype(jnp.float32)
    return beta_two * second.astype(jnp.float32) + (1.0 - beta_two) * grad_wide * grad_wide


def updated_of(weight, gradient, first, second):
    return (
        weight.astype(jnp.float32)
        - learn_rate * first_of(gradient, first) / (jnp.sqrt(second_of(gradient, second)) + adam_eps)
    ).astype(jnp.bfloat16)


def grid_of(experts):
    columns = 1 << ((experts.bit_length() - 1) // 2)
    return experts // columns, columns


def swap(axis, mask, value):
    count = lax.axis_size(axis)
    return lax.ppermute(value, axis, [(i, i ^ mask) for i in range(count)])


def spread(axis, masks, blocks):
    return blocks + [swap(axis, mask, block) for mask in masks for block in blocks]


def pick(index, choices):
    out = choices[0]
    for at, choice in enumerate(choices[1:], 1):
        out = jnp.where(index == at, choice, out)
    return out


def ring_of(layers):
    return list(range(0, layers, 2)) + list(range(1, layers, 2))[::-1]


def ring_step(block, layers, columns):
    ring = ring_of(layers)
    return lax.ppermute(
        block,
        "expert",
        [(k * columns + x, to * columns + x) for k, to in zip(ring, ring[1:] + ring[:1]) for x in range(columns)],
    )


def weighted_products(blocks, weights, scale, prior=None, kept=None):
    count, many = len(blocks), len(weights)
    rows, depth = blocks[0].shape
    wide = weights[0].shape[1]
    steps = count // 2
    pair = 2 * rows
    extra = 0 if prior is None else 1

    def body(*refs):
        sources, held, scales = refs[:count], refs[count : count + many], refs[count + many]
        outs = refs[count + many + 1 + extra : -2]
        window, arrived = refs[-2:]

        def fetch(step, slot):
            for at in range(steps):

                @pl.when(step == at)
                def _():
                    for side in (0, 1):
                        pltpu.make_async_copy(
                            sources[2 * at + side], window.at[slot, pl.ds(side * rows, rows)], arrived.at[slot, side]
                        ).start()

        fetch(0, 0)

        def run(step, carry):
            slot = lax.rem(step, 2)
            fetch(step + 1, 1 - slot)
            for side in (0, 1):
                pltpu.make_async_copy(
                    sources[0], window.at[slot, pl.ds(side * rows, rows)], arrived.at[slot, side]
                ).wait()
            here = pl.ds(pl.multiple_of(step * pair, pair), pair)
            total = refs[count + many + 1][here, :] if extra else jnp.zeros((pair, wide), jnp.float32)
            for at in range(many):
                value = jnp.dot(window[slot], held[at][...], preferred_element_type=jnp.float32)
                act = (value / (1.0 + jnp.exp(-value))).astype(jnp.bfloat16).astype(jnp.float32)
                total = total + scales[here, at : at + 1] * act
            if kept is None:
                outs[0][here, :] = total
            else:

                @pl.when(step < kept // 2)
                def _():
                    outs[0][here, :] = total

                @pl.when(step >= kept // 2)
                def _():
                    there = pl.ds(pl.multiple_of((step - kept // 2) * pair, pair), pair)
                    outs[1][there, :] = total.astype(jnp.bfloat16)

            return carry

        lax.fori_loop(0, steps, run, None)

    near = pl.BlockSpec(memory_space=pltpu.VMEM)
    if kept is None:
        shapes = jax.ShapeDtypeStruct((count * rows, wide), jnp.float32)
    else:
        shapes = (
            jax.ShapeDtypeStruct((kept * rows, wide), jnp.float32),
            jax.ShapeDtypeStruct(((count - kept) * rows, wide), jnp.bfloat16),
        )
    return pl.pallas_call(
        body,
        out_shape=shapes,
        in_specs=[pl.BlockSpec(memory_space=pl.ANY)] * count + [near] * (many + 1 + extra),
        out_specs=near if kept is None else (near, near),
        scratch_shapes=[pltpu.VMEM((2, pair, depth), jnp.bfloat16), pltpu.SemaphoreType.DMA((2, 2))],
        compiler_params=pltpu.CompilerParams(vmem_limit_bytes=60 << 20),
        cost_estimate=pl.CostEstimate(
            flops=2 * count * rows * depth * wide * many,
            bytes_accessed=2 * (count * rows * depth + many * depth * wide),
            transcendentals=count * rows * wide * many,
        ),
    )(*blocks, *weights, scale, *([] if prior is None else [prior]))


def tie(*values):
    return lax.optimization_barrier(values)


def at_index(vector, index):
    index = jnp.asarray(index)
    places = jnp.arange(vector.shape[0], dtype=jnp.int32)
    return jnp.sum(jnp.where(index[..., None] == places, vector, 0), axis=-1)


def two_rounds(placement, hosting, layers):
    ids = jnp.arange(2 * layers, dtype=jnp.int32)
    beside = at_index(placement, hosting ^ 1)
    step = at_index(beside, ids ^ 1)
    lowest, reach = ids, ids
    for _ in range(layers - 1):
        reach = at_index(step, reach)
        lowest = jnp.minimum(lowest, reach)
    late = (lowest > at_index(lowest, ids ^ 1)).astype(jnp.int32)
    late_pairs = late.reshape(layers, 2)
    host_pairs = hosting.reshape(layers, 2)
    rounds = []
    for turn in (0, 1):
        column = jnp.where(late_pairs[:, 0] == turn, 0, 1)
        host = jnp.where(column == 0, host_pairs[:, 0], host_pairs[:, 1])
        rounds.append((column, host // 2, host % 2))
    return rounds


class Rounds:
    def __init__(self, placement, hosting, layers, z, x):
        perms = list(itertools.permutations(range(layers)))
        table = jnp.array(perms, jnp.int32)
        self.x = x
        self.perms = perms
        rounds = two_rounds(placement, hosting, layers)
        numbers, stays = [], []
        for _, target, _ in rounds:
            match = jnp.all(table == target[None, :], axis=1)
            numbers.append(jnp.sum(jnp.where(match, jnp.arange(len(perms), dtype=jnp.int32), 0)))
            stays.append(at_index(target, z) == z)
        mine_first = at_index(rounds[0][0], z) == x
        first_is_mine = jnp.sum(jnp.where(rounds[0][1] == z, rounds[0][2], 0)) == x
        self.plan = (numbers, stays, mine_first, first_is_mine)

    def halves(self, state):
        rows = state.shape[0] // 2
        kept = lax.dynamic_slice_in_dim(state, self.x * rows, rows, axis=0)
        given = lax.dynamic_slice_in_dim(state, (1 - self.x) * rows, rows, axis=0)
        return kept, given

    def blocks(self, kept, taken):
        _, _, mine_first, _ = self.plan
        return jnp.where(mine_first, kept, taken), jnp.where(mine_first, taken, kept)

    def move(self, turn, block, beside=lambda: ()):
        def branch(perm):
            pairs = [(2 * k + c, 2 * to + c) for k, to in enumerate(perm) for c in (0, 1) if to != k]

            def run(block):
                moved = lax.ppermute(block, "expert", pairs) if pairs else block
                return (moved,) + tuple(beside())

            return run

        return lax.switch(self.plan[0][turn], [branch(perm) for perm in self.perms], block)

    def pass_on(self, blocks, moved):
        _, stays, _, first_is_mine = self.plan
        landed = [jnp.where(stay, block, came) for stay, block, came in zip(stays, blocks, moved)]
        other = jnp.where(first_is_mine, landed[1], landed[0])
        other, blocks, moved = tie(other, blocks, moved)
        landed = [jnp.where(stay, block, came) for stay, block, came in zip(stays, blocks, moved)]
        return jnp.where(first_is_mine, landed[0], landed[1]), other

    def join(self, own, came):
        top = jnp.where(self.x == 0, own, came)
        bottom = jnp.where(self.x == 0, came, own)
        return jnp.concatenate([top, bottom], axis=0)


def migrate_by_pieces(moments, placement, experts):
    results = []
    for moment in moments:
        pieces = moment.reshape(experts, moment.shape[0] // experts, moment.shape[1])
        pieces = lax.all_to_all(pieces, "expert", split_axis=0, concat_axis=0, tiled=True)
        pieces = jnp.take(pieces, placement, axis=0)
        pieces = lax.all_to_all(pieces, "expert", split_axis=0, concat_axis=0, tiled=True)
        results.append(pieces.reshape(moment.shape))
    return results


def shards(
    tokens, routes, route_weights, placement, expert_weights, grads, first_moment, second_moment
):
    experts = lax.axis_size("expert")
    layers, columns = grid_of(experts)
    dp_count = lax.axis_size("dp")
    me = lax.axis_index("expert")
    z, x = me // columns, me % columns
    dp_index = lax.axis_index("dp")
    expert_ids = jnp.arange(experts, dtype=jnp.int32)
    tok_count = tokens.shape[0]
    shard = expert_weights.shape[2]

    x_masks = list(range(1, columns))
    y_masks = [CORES * k for k in range(1, dp_count // CORES)]
    y_count = dp_count // CORES
    by_rounds = columns == 2 and layers == 4

    hosting = jnp.sum(
        jnp.where(placement[None, :] == expert_ids[:, None], expert_ids[None, :], 0), axis=1
    )
    ring = ring_of(layers)
    layer_in = [
        sum(jnp.where(z == k, ring[(at - back) % layers], 0) for at, k in enumerate(ring)) for back in range(layers)
    ]
    state = (grads[0], first_moment[0], second_moment[0])

    updated = updated_of(expert_weights[0], *state)
    slots = [updated, ring_step(updated, layers, columns)]
    if by_rounds:
        updated, tokens = tie(updated, tokens)
    by_x = [swap("expert", mask, tokens) for mask in x_masks]
    by_y = [swap("dp", mask, tokens) for mask in y_masks]
    by_core = swap("dp", 1, tokens)
    named = jnp.sum(
        jnp.where(routes[:, :, None] == expert_ids[None, None, :], route_weights[:, :, None], 0.0), axis=1
    )
    factors = jnp.stack(spread("dp", [1], [named]))
    sources = [at_index(placement, me ^ mask) for mask in range(columns)]
    source_slots = [
        sum(jnp.where(layer_in[at] == source // columns, at, 0) for at in range(layers)) for source in sources
    ]
    came_from = sources[0] % columns ^ x
    if by_rounds:
        rounds = Rounds(placement, hosting, layers, z, x)
        kept, given = zip(*[rounds.halves(member) for member in state])
        given = jnp.concatenate([first_of(given[0], given[1]), second_of(given[0], given[2])]).astype(jnp.bfloat16)
        kept = jnp.concatenate([first_of(kept[0], kept[1]), second_of(kept[0], kept[2])]).astype(jnp.bfloat16)
        slots, factors, kept, given, rounds.plan, source_slots, came_from = tie(
            slots, factors, kept, given, rounds.plan, source_slots, came_from
        )
    else:
        moments = (first_of(state[0], state[1]).astype(jnp.bfloat16), second_of(state[0], state[2]).astype(jnp.bfloat16))
        new_first, new_second = migrate_by_pieces(moments, placement, experts)

    slots.append(ring_step(slots[1], layers, columns))
    by_xy = [swap("dp", mask, block) for block in by_x for mask in y_masks]
    far = [by_core] + [swap("dp", 1, block) for block in by_y + by_x]
    factors = jnp.stack(spread("dp", y_masks, [factors]))
    if by_rounds:
        taken = swap("expert", 1, given)
        slots, by_xy, far, factors, taken = tie(slots, by_xy, far, factors, taken)

    while len(slots) < layers:
        slots.append(ring_step(slots[-1], layers, columns))
    far = far + [swap("dp", 1, block) for block in by_xy]
    factors = jnp.stack(spread("expert", x_masks, [factors]))
    blocks = []
    for near in ([tokens] + by_y + by_x + by_xy, far):
        mine, others = near[:y_count], near[y_count:]
        by_x_part, by_xy_part = others[: columns - 1], others[columns - 1 :]
        per_x = [mine] + [
            [by_x_part[at]] + by_xy_part[at * (y_count - 1) : (at + 1) * (y_count - 1)] for at in range(columns - 1)
        ]
        blocks.append(per_x)
    blocks = [blocks[core][xs][ys] for xs in range(columns) for core in range(CORES) for ys in range(y_count)]
    factors = factors.transpose(0, 2, 1, 3, 4).reshape(len(blocks) * tok_count, experts)
    scale = jnp.stack(
        [
            jnp.sum(jnp.where(expert_ids[None, :] == layer * columns + x, factors, 0.0), axis=1)
            for layer in layer_in
        ],
        axis=1,
    )
    early = min(3, layers - 1)
    partial = weighted_products(blocks, slots[:early], scale[:, :early])
    scale = jnp.pad(scale[:, early:], ((0, 0), (0, 128 - layers + early)))
    found = [pick(number, slots[:early]) for number in source_slots]
    if by_rounds:
        most = kept.shape[0] * 3 // 4
        first = rounds.blocks(kept[:most], taken[:most])
        second = rounds.blocks(kept[most:], taken[most:])
        slots, first, second, partial, scale, found = tie(slots, first, second, partial, scale, found)

    def needed(mask):
        out = found[mask]
        for at in range(early, layers):
            out = jnp.where(source_slots[mask] == at, slots[at], out)
        return out

    came = [swap("expert", mask, needed(mask)) for mask in x_masks]

    def finish():
        return weighted_products(blocks, slots[early:], scale, partial, len(blocks) // columns)

    def give(others):
        others = others.reshape(columns - 1, -1, shard)
        return [swap("expert", mask, others[at]) for at, mask in enumerate(x_masks)]

    if by_rounds:
        total, others = finish()
        first, second, total, others = tie(first, second, total, others)
        (one,) = rounds.move(0, first[0])
        one, first, second, others = tie(one, first, second, others)
        two, *returned = rounds.move(1, first[1], lambda: give(others))
        one, two, second, came = tie(one, two, second, came)
        most_own, most_other = rounds.pass_on(first, (one, two))

        most_came = swap("expert", 1, most_other)
        (one,) = rounds.move(0, second[0])
        one, second = tie(one, second)
        (two,) = rounds.move(1, second[1])
        one, two, returned, total = tie(one, two, returned, total)
        rest_own, rest_other = rounds.pass_on(second, (one, two))
        rest_came = swap("expert", 1, rest_other)
    else:
        total, others = finish()
        returned = give(others)

    for block in returned:
        total = total + block.astype(jnp.float32)
    total = total.astype(jnp.bfloat16).reshape(CORES, y_count, tok_count, shard)
    pieces = [None] * dp_count
    for core in range(CORES):
        for ys in range(y_count):
            mask = ys * CORES + core
            piece = total[core, ys]
            pieces[mask] = piece if mask == 0 else swap("dp", mask, piece)
    new_weights = needed(0)
    for mask, block in zip(x_masks, came):
        new_weights = jnp.where(came_from == mask, block, new_weights)
    bit = 1
    while bit < dp_count:
        turned = (dp_index & bit) != 0
        pieces = [jnp.where(turned, pieces[i ^ bit], pieces[i]) for i in range(dp_count)]
        bit *= 2
    mixed = jnp.concatenate(pieces, axis=1)
    if by_rounds:
        half = kept.shape[0] // 2
        new_first = rounds.join(most_own[:half], most_came[:half])
        new_second = rounds.join(
            jnp.concatenate([most_own[half:], rest_own]), jnp.concatenate([most_came[half:], rest_came])
        )
    return (new_weights[None], new_first[None], new_second[None], mixed)


def solution(mesh):
    return jax.shard_map(
        shards,
        mesh=mesh,
        in_specs=(
            P(("dp", "expert"), None),
            P(("dp", "expert"), None),
            P(("dp", "expert"), None),
            P(),
            P("expert", None, "dp"),
            P("expert", None, "dp"),
            P("expert", None, "dp"),
            P("expert", None, "dp"),
        ),
        out_specs=(
            P("expert", None, "dp"),
            P("expert", None, "dp"),
            P("expert", None, "dp"),
            P(("dp", "expert"), None),
        ),
        check_vma=False,
    )
```
